32 devices in a mesh: groups: 2 (over y), spec: 4 (over z), band: 2 (over x), sub: 2 (over core).
Axes of the slice: x: 2, y: 2, z: 4, core: 2. Of those that a mesh axis runs over, the one named last changes fastest.
Arguments:
- spectrum: float32 [3456, 32, 512], P(('groups', 'spec'), 'band', 'sub'), parts along dimension 0, may hold values from 0.05 to 2
- wind_speed: float32 [4, 2, 4, 1024], P(('groups', 'band'), 'sub', 'spec'), parts along dimension 0, may hold values from 3 to 25
- wind_dir: float32 [4, 2, 4, 1024], P(('groups', 'band'), 'sub', 'spec'), parts along dimension 0, may hold values from -3.140625 to 3.140625
- ice_mask: int32 [4, 2, 4, 1024], P(('groups', 'band'), 'sub', 'spec'), parts along dimension 0, may hold values 0 or 1
- depth_class: int32 [4, 2, 4, 1024], P(('groups', 'band'), 'sub', 'spec'), parts along dimension 0, may hold values from 0 to 15
- bottom_table: float32 [16, 48], replicated, may hold values from 0.01 to 0.2
- sea_slots: int32 [4, 2, 4, 768], P(('groups', 'band'), 'sub', 'spec'), parts along dimension 0, may hold values from 0 to 1023, as said below
- sea_count: int32 [4, 2, 4, 1], P(('groups', 'band'), 'sub', 'spec'), parts along dimension 0, may hold values from 341 to 768, as said below
Outputs:
- advanced: float32 [3456, 32, 512], P(('groups', 'spec'), 'band', 'sub'), parts along dimension 0
The draws below stay inside these ranges and needn't reach their ends.
There are 2 independent parts, one for each index of `groups`. The reference program is written for one: setup_inputs(seed, part) draws one part's arguments, and reference() takes and returns one part's arrays. A program takes and returns all parts, laid end to end along the dimension named above; an argument that names none is the same for every part. Nothing has to cross between parts.
Inputs may be any that keep to these rules, and one draw needn't show every extreme that they name: `sea_slots`: the 768 entries of one block's row are distinct positions of that block. `sea_count`: some block holds exactly 768 sea points.
All inputs are finite; a program needn't handle non-finite values. No bound on the sum of `ice_mask` on one device may be relied on, other than what follows from the above.
Results may differ from the reference program's by a relative error of at most 0.0003.
Values sent between devices are 32-bit elements; how exact they have to be, the bound alone decides.
A program may use at most 128 MiB of HBM per device.

```python
import math
import jax
import jax.numpy as jnp
from jax import lax

ND = 36
NF = 48
NDEPTH = 16
LAT_DEV = 16
LON_DEV = 256
K = 1728
NLAT = 32
NLON = 512
PSRC = 1024
SEA_MOST = 768
N_SPEC = 4
N_BAND = 2
N_SUB = 2


def draw_sea_slots(key, part):
    key = jax.random.fold_in(key, 11)
    block_total = N_BAND * N_SUB * N_SPEC
    scores = jax.random.randint(key, (block_total, PSRC), 0, 2 ** 20) * PSRC + jnp.arange(PSRC, dtype=jnp.int32)[None, :]
    ordered = jnp.argsort(scores, axis=-1, stable=True)[:, :SEA_MOST]
    return ordered.astype(jnp.int32).reshape(N_BAND, N_SUB, N_SPEC, SEA_MOST)


def draw_sea_count(key, part):
    key = jax.random.fold_in(key, 12)
    counts = jax.random.randint(key, (N_BAND, N_SUB, N_SPEC, 1), PSRC // 3, SEA_MOST + 1)
    return counts.at[0, 0, 0, 0].set(SEA_MOST).astype(jnp.int32)


def with_ends(result, key, least, top_value):
    extent = result.shape
    place = [jax.random.randint(jax.random.fold_in(key, axis), (), 0, extent[axis]) for axis in range(len(extent))]
    result = result.at[tuple(place)].set(least)
    longest = extent.index(max(extent))
    place[longest] = (place[longest] + 1) % extent[longest]
    return result.at[tuple(place)].set(top_value)


def levels(own_key, dims, split, smallest, largest):
    gain = 1.0
    for axis_at, parts in split:
        heights = jax.random.uniform(jax.random.fold_in(jax.random.fold_in(own_key, 6), axis_at), (parts,), jnp.float32, smallest / len(split), largest / len(split))
        gain = gain * jnp.repeat(jnp.exp(heights), dims[axis_at] // parts).reshape((-1,) + (1,) * (len(dims) - 1 - axis_at))
    return gain


def setup_inputs(seed: int = 0, part: int = 0) -> dict:
    key_list = jax.random.split(jax.random.key(seed), 9)
    part_keys = jax.random.split(jax.random.fold_in(key_list[8], part), 9)
    return {
        "spectrum": jnp.clip(jnp.exp(math.log(2.0) - 3.6888794 * jax.random.uniform(part_keys[0], (K, NLAT, NLON), jnp.float32) ** levels(part_keys[0], (K, NLAT, NLON), ((0, 4), (1, 2), (2, 2)), -0.2, 0.2)), 0.05, 2.0),
        "wind_speed": jnp.clip(3.0 + 22.0 * jax.random.uniform(part_keys[1], (N_BAND, N_SUB, N_SPEC, PSRC), jnp.float32) ** levels(part_keys[1], (N_BAND, N_SUB, N_SPEC, PSRC), ((0, 2), (1, 2), (2, 4)), -0.2, 0.2), 3.0, 25.0),
        "wind_dir": jnp.clip(jax.random.uniform(part_keys[2], (N_BAND, N_SUB, N_SPEC, PSRC), jnp.float32, -3.140625, 3.140625), -3.140625, 3.140625),
        "ice_mask": with_ends((jax.random.randint(part_keys[3], (N_BAND, N_SUB, N_SPEC, PSRC), 0, 4) < 1).astype(jnp.int32), jax.random.fold_in(part_keys[3], 1), 0, 1),
        "depth_class": with_ends(jax.random.randint(part_keys[4], (N_BAND, N_SUB, N_SPEC, PSRC), 0, NDEPTH), jax.random.fold_in(part_keys[4], 1), 0, NDEPTH - 1).astype(jnp.int32),
        "bottom_table": jnp.clip(jnp.exp(jax.random.uniform(key_list[5], (NDEPTH, NF), jnp.float32, math.log(0.01), math.log(0.2))), 0.01, 0.2),
        "sea_slots": draw_sea_slots(jax.random.fold_in(jax.random.fold_in(key_list[8], part), 71), part),
        "sea_count": draw_sea_count(jax.random.fold_in(jax.random.fold_in(key_list[8], part), 71), part),
    }


low_frequency = 0.04
growth_ratio = 1.07
courant_limit = 0.44
gravity = 9.81
wind_coef = 0.02
dissip_coef = 0.03
steep_ref = 0.4
quad_coef = 0.02
ice_rate = 0.5


def frequencies(index):
    return low_frequency * jnp.exp(index * math.log(growth_ratio))


def shifted(values, dir_turn, offset):
    rolled = jnp.roll(values, dir_turn, axis=0)
    count_freqs = values.shape[1]
    if offset > 0:
        padding = jnp.zeros((values.shape[0], offset) + values.shape[2:], values.dtype)
        return jnp.concatenate([padding, rolled[:, :count_freqs - offset]], axis=1)
    padding = jnp.zeros((values.shape[0], -offset) + values.shape[2:], values.dtype)
    return jnp.concatenate([rolled[:, -offset:], padding], axis=1)


def source_step(spectrum, wind_speed, wind_dir, ice_flag, depth_class, sea_flag, bottom_table):
    count_dirs, count_freqs = spectrum.shape[0], spectrum.shape[1]
    frequency = frequencies(jnp.arange(count_freqs, dtype=jnp.float32))
    bin_width = frequency * (growth_ratio - 1.0 / growth_ratio) * 0.5 * (2.0 * math.pi / count_dirs)
    angles = jnp.arange(count_dirs, dtype=jnp.float32) * (2.0 * math.pi / count_dirs)
    energy_sum = jnp.sum(spectrum * bin_width[None, :, None], axis=(0, 1))
    inverse_sum = jnp.sum(spectrum * (bin_width / frequency)[None, :, None], axis=(0, 1))
    mean_freq = energy_sum / inverse_sum
    mean_wave = mean_freq * mean_freq * (4.0 * math.pi ** 2 / gravity)
    steepness = energy_sum * mean_wave * mean_wave
    ice_float = ice_flag.astype(jnp.float32)
    open_water = 1.0 - ice_float
    inverse_speed = frequency * (2.0 * math.pi / gravity)
    alignment = jnp.cos(angles[:, None] - wind_dir[None, :])
    wind_ratio = wind_speed[None, None, :] * inverse_speed[None, :, None] * alignment[:, None, :]
    wind_growth = wind_coef * jnp.maximum(wind_ratio - 1.0, 0.0) * open_water[None, None, :]
    dissipation = dissip_coef * (frequency[:, None] / mean_freq[None, :]) * (steepness / steep_ref)[None, :] ** 2 * open_water[None, :]
    one_hot = (depth_class[None, :] == jnp.arange(bottom_table.shape[0], dtype=jnp.int32)[:, None]).astype(jnp.float32)
    friction = jnp.dot(bottom_table.T, one_hot, precision=lax.Precision.HIGHEST)
    net_rate = wind_growth - dissipation[None] - friction[None]
    weights = (quad_coef * (frequency / frequency[-1]) ** 2)[None, :, None]
    center_sq = spectrum * spectrum
    plus_one = shifted(spectrum, -1, -3)
    minus_one = shifted(spectrum, 3, 4)
    plus_two = shifted(spectrum, 1, -3)
    minus_two = shifted(spectrum, -3, 4)
    quad_one = weights * (center_sq * (plus_one / 2.4414 + minus_one / 0.3164) - 2.0 * spectrum * plus_one * minus_one / 0.7725)
    quad_two = weights * (center_sq * (plus_two / 2.4414 + minus_two / 0.3164) - 2.0 * spectrum * plus_two * minus_two / 0.7725)
    transfer = -2.0 * (quad_one + quad_two) + shifted(quad_one, 1, 3) + shifted(quad_one, -3, -4) + shifted(quad_two, -1, 3) + shifted(quad_two, 3, -4)
    updated = jnp.maximum(spectrum * (1.0 + net_rate) + transfer, 0.0)
    damping = jnp.exp(-ice_rate * (frequency / frequency[-1]) ** 2)
    ice_factor = 1.0 - ice_float[None, :] * (1.0 - damping[:, None])
    return updated * ice_factor[None] * sea_flag[None, None, :]


def courant_numbers(dir_index, freq_index, latitude, count_dirs):
    ratio = low_frequency / frequencies(freq_index)
    angle = dir_index * (2.0 * math.pi / count_dirs)
    courant_x = courant_limit * (ratio * jnp.cos(angle))[:, None] / jnp.cos(latitude)[None, :]
    courant_y = courant_limit * ratio * jnp.sin(angle)
    return courant_x, courant_y


def latitudes(row_index, total_rows):
    degrees = -60.0 + 120.0 * (row_index + 0.5) / total_rows
    return degrees * (math.pi / 180.0)


def upwind_step(padded, courant_x, courant_y):
    center = padded[:, 1:-1, 1:-1]
    east = padded[:, 1:-1, 2:]
    west = padded[:, 1:-1, :-2]
    north = padded[:, 2:, 1:-1]
    south = padded[:, :-2, 1:-1]
    east_go = jnp.maximum(courant_x, 0.0)[:, :, None]
    west_go = jnp.minimum(courant_x, 0.0)[:, :, None]
    north_go = jnp.maximum(courant_y, 0.0)[:, None, None]
    south_go = jnp.minimum(courant_y, 0.0)[:, None, None]
    flux_east = east_go * center + west_go * east
    flux_west = east_go * west + west_go * center
    flux_north = north_go * center + south_go * north
    flux_south = north_go * south + south_go * center
    return center - (flux_east - flux_west) - (flux_north - flux_south)


def reference(spectrum, wind_speed, wind_dir, ice_mask, depth_class, bottom_table, sea_slots, sea_count):
    block_count = N_BAND * N_SUB
    per_device = LAT_DEV * LON_DEV
    live = (jnp.arange(SEA_MOST, dtype=jnp.int32)[None, None, None, :] < sea_count).astype(jnp.float32)
    flat_slots = sea_slots.reshape(-1, SEA_MOST)
    sea_blocks = jax.vmap(lambda slot_row, live_row: jnp.zeros((PSRC,), jnp.float32).at[slot_row].set(live_row))(flat_slots, live.reshape(-1, SEA_MOST))
    sea_dev = sea_blocks.reshape(block_count, per_device)
    blocked = spectrum.reshape(K, N_BAND, LAT_DEV, N_SUB, LON_DEV).transpose(1, 3, 0, 2, 4).reshape(block_count, ND, NF, per_device)

    def one_block(items):
        spec_block, speed_row, dir_row, ice_row, depth_row, sea_row = items
        return source_step(spec_block, speed_row, dir_row, ice_row, depth_row, sea_row, bottom_table)

    sourced = lax.map(one_block, (blocked, wind_speed.reshape(block_count, per_device), wind_dir.reshape(block_count, per_device), ice_mask.reshape(block_count, per_device), depth_class.reshape(block_count, per_device), sea_dev))
    grid = sourced.reshape(N_BAND, N_SUB, K, LAT_DEV, LON_DEV).transpose(2, 0, 3, 1, 4).reshape(ND, NF, NLAT, NLON)
    sea_grid = sea_dev.reshape(N_BAND, N_SUB, LAT_DEV, LON_DEV).transpose(0, 2, 1, 3).reshape(NLAT, NLON)
    latitude = latitudes(jnp.arange(NLAT, dtype=jnp.float32), NLAT)
    freq_index = jnp.arange(NF, dtype=jnp.float32)

    def one_direction(items):
        plane, dir_value = items
        courant_x, courant_y = courant_numbers(jnp.full((NF,), dir_value), freq_index, latitude, ND)
        padded = jnp.pad(plane, ((0, 0), (1, 1), (0, 0)))
        padded = jnp.pad(padded, ((0, 0), (0, 0), (1, 1)), mode="wrap")
        return upwind_step(padded, courant_x, courant_y) * sea_grid[None]

    moved = lax.map(one_direction, (grid, jnp.arange(ND, dtype=jnp.float32)))
    return moved.reshape(K, NLAT, NLON)
```

```python
import math

import functools

import jax
import jax.numpy as jnp
import numpy as np
from jax import lax
from jax.experimental import pallas as pl
from jax.experimental.pallas import tpu as pltpu
from jax.sharding import PartitionSpec as P

ND = 36
NF = 48


low_frequency = 0.04
growth_ratio = 1.07
courant_limit = 0.44
gravity = 9.81
wind_coef = 0.02
dissip_coef = 0.03
steep_ref = 0.4
quad_coef = 0.02
ice_rate = 0.5


def with_halo(block, sides, width, periodic):
    for axis, dim in sides:
        count = lax.axis_size(axis)
        forward = [(i, i + 1) for i in range(count - 1)]
        if periodic:
            forward.append((count - 1, 0))
        backward = [(target, source) for source, target in forward]
        low = lax.ppermute(
            lax.slice_in_dim(block, block.shape[dim] - width, None, axis=dim), axis, forward
        )
        high = lax.ppermute(lax.slice_in_dim(block, 0, width, axis=dim), axis, backward)
        block = jnp.concatenate([low, block, high], axis=dim)
    return block


def frequencies(index):
    return low_frequency * jnp.exp(index * math.log(growth_ratio))


def shifted(values, dir_turn, offset):
    rolled = jnp.roll(values, dir_turn, axis=0)
    count_freqs = values.shape[1]
    if offset > 0:
        padding = jnp.zeros((values.shape[0], offset) + values.shape[2:], values.dtype)
        return jnp.concatenate([padding, rolled[:, : count_freqs - offset]], axis=1)
    padding = jnp.zeros((values.shape[0], -offset) + values.shape[2:], values.dtype)
    return jnp.concatenate([rolled[:, -offset:], padding], axis=1)


def source_step(spectrum, wind_speed, wind_dir, ice_flag, depth_class, sea_flag, bottom_table):
    count_dirs, count_freqs = (spectrum.shape[0], spectrum.shape[1])
    frequency = frequencies(jnp.arange(count_freqs, dtype=jnp.float32))
    bin_width = frequency * (growth_ratio - 1.0 / growth_ratio) * 0.5 * (2.0 * math.pi / count_dirs)
    angles = jnp.arange(count_dirs, dtype=jnp.float32) * (2.0 * math.pi / count_dirs)
    energy_sum = jnp.sum(spectrum * bin_width[None, :, None], axis=(0, 1))
    inverse_sum = jnp.sum(spectrum * (bin_width / frequency)[None, :, None], axis=(0, 1))
    mean_freq = energy_sum / inverse_sum
    mean_wave = mean_freq * mean_freq * (4.0 * math.pi**2 / gravity)
    steepness = energy_sum * mean_wave * mean_wave
    ice_float = ice_flag.astype(jnp.float32)
    open_water = 1.0 - ice_float
    inverse_speed = frequency * (2.0 * math.pi / gravity)
    alignment = jnp.cos(angles[:, None] - wind_dir[None, :])
    wind_ratio = wind_speed[None, None, :] * inverse_speed[None, :, None] * alignment[:, None, :]
    wind_growth = wind_coef * jnp.maximum(wind_ratio - 1.0, 0.0) * open_water[None, None, :]
    dissipation = (
        dissip_coef
        * (frequency[:, None] / mean_freq[None, :])
        * (steepness / steep_ref)[None, :] ** 2
        * open_water[None, :]
    )
    one_hot = (
        depth_class[None, :] == jnp.arange(bottom_table.shape[0], dtype=jnp.int32)[:, None]
    ).astype(jnp.float32)
    friction = jnp.dot(bottom_table.T, one_hot, precision=lax.Precision.HIGHEST)
    net_rate = wind_growth - dissipation[None] - friction[None]
    weights = (quad_coef * (frequency / frequency[-1]) ** 2)[None, :, None]
    center_sq = spectrum * spectrum
    plus_one = shifted(spectrum, -1, -3)
    minus_one = shifted(spectrum, 3, 4)
    plus_two = shifted(spectrum, 1, -3)
    minus_two = shifted(spectrum, -3, 4)
    quad_one = weights * (
        center_sq * (plus_one / 2.4414 + minus_one / 0.3164)
        - 2.0 * spectrum * plus_one * minus_one / 0.7725
    )
    quad_two = weights * (
        center_sq * (plus_two / 2.4414 + minus_two / 0.3164)
        - 2.0 * spectrum * plus_two * minus_two / 0.7725
    )
    transfer = (
        -2.0 * (quad_one + quad_two)
        + shifted(quad_one, 1, 3)
        + shifted(quad_one, -3, -4)
        + shifted(quad_two, -1, 3)
        + shifted(quad_two, 3, -4)
    )
    updated = jnp.maximum(spectrum * (1.0 + net_rate) + transfer, 0.0)
    damping = jnp.exp(-ice_rate * (frequency / frequency[-1]) ** 2)
    ice_factor = 1.0 - ice_float[None, :] * (1.0 - damping[:, None])
    return updated * ice_factor[None] * sea_flag[None, None, :]


def courant_numbers(dir_index, freq_index, latitude, count_dirs):
    ratio = low_frequency / frequencies(freq_index)
    angle = dir_index * (2.0 * math.pi / count_dirs)
    courant_x = courant_limit * (ratio * jnp.cos(angle))[:, None] / jnp.cos(latitude)[None, :]
    courant_y = courant_limit * ratio * jnp.sin(angle)
    return (courant_x, courant_y)


def latitudes(row_index, total_rows):
    degrees = -60.0 + 120.0 * (row_index + 0.5) / total_rows
    return degrees * (math.pi / 180.0)


def upwind_step(padded, courant_x, courant_y):
    center = padded[:, 1:-1, 1:-1]
    east = padded[:, 1:-1, 2:]
    west = padded[:, 1:-1, :-2]
    north = padded[:, 2:, 1:-1]
    south = padded[:, :-2, 1:-1]
    east_go = jnp.maximum(courant_x, 0.0)[:, :, None]
    west_go = jnp.minimum(courant_x, 0.0)[:, :, None]
    north_go = jnp.maximum(courant_y, 0.0)[:, None, None]
    south_go = jnp.minimum(courant_y, 0.0)[:, None, None]
    flux_east = east_go * center + west_go * east
    flux_west = east_go * west + west_go * center
    flux_north = north_go * center + south_go * north
    flux_south = north_go * south + south_go * center
    return center - (flux_east - flux_west) - (flux_north - flux_south)


def body(spectrum, wind_speed, wind_dir, ice_mask, depth_class, bottom_table, sea_slots, sea_count):
    local_comps, rows, cols = spectrum.shape
    spec_size = lax.axis_size("spec")
    block_len = rows * cols // spec_size
    most = sea_slots.shape[-1]
    all_slots, all_counts = (
        lax.all_gather(sea_slots, "spec", axis=2, tiled=True),
        lax.all_gather(sea_count, "spec", axis=2, tiled=True),
    )
    all_slots = all_slots.reshape(spec_size, most)
    all_counts = all_counts.reshape(spec_size, 1)
    slot_range = jnp.arange(most, dtype=jnp.int32)
    all_live = (slot_range[None, :] < all_counts).astype(jnp.float32)
    block_rows = jnp.arange(spec_size, dtype=jnp.int32)[:, None]
    sea_prop = (
        jnp.zeros((spec_size, block_len), jnp.float32).at[block_rows, all_slots].set(all_live)
    )
    my_slots = sea_slots.reshape(most)
    my_live = (slot_range < sea_count.reshape(())).astype(jnp.float32)
    speed_row = wind_speed.reshape(block_len)
    dir_row = wind_dir.reshape(block_len)
    ice_row = ice_mask.reshape(block_len)
    depth_row = depth_class.reshape(block_len)
    blocks = spectrum.reshape(local_comps, spec_size, block_len)
    gathered = lax.all_to_all(blocks, "spec", split_axis=1, concat_axis=0, tiled=True)
    sea_own = jnp.zeros((block_len,), jnp.float32).at[my_slots].set(my_live)
    sourced = source_step(
        gathered.reshape(ND, NF, block_len),
        speed_row,
        dir_row,
        ice_row,
        depth_row,
        sea_own,
        bottom_table,
    )
    stepped = lax.all_to_all(
        sourced.reshape(ND * NF, 1, block_len), "spec", split_axis=0, concat_axis=1, tiled=True
    )
    grid_part = stepped.reshape(local_comps, rows, cols)
    with_rows = with_halo(grid_part, (("band", 1),), 1, False)
    padded = with_halo(with_rows, (("sub", 2),), 1, True)
    comp_index = lax.axis_index("spec") * local_comps + jnp.arange(local_comps, dtype=jnp.int32)
    dir_index = (comp_index // NF).astype(jnp.float32)
    freq_index = (comp_index % NF).astype(jnp.float32)
    row_index = (lax.axis_index("band") * rows + jnp.arange(rows, dtype=jnp.int32)).astype(
        jnp.float32
    )
    latitude = latitudes(row_index, rows * lax.axis_size("band"))
    courant_x, courant_y = courant_numbers(dir_index, freq_index, latitude, ND)
    moved = upwind_step(padded, courant_x, courant_y)
    return moved * sea_prop.reshape(rows, cols)[None]


REACH = 4
PAD = 7
MESH = pl.DeviceIdType.MESH
UNIT = (growth_ratio - 1.0 / growth_ratio) * 0.5 * (2.0 * math.pi / ND)


def frequency_table():
    n = np.arange(-PAD, NF + PAD, dtype=np.float64)
    f = low_frequency * growth_ratio**n
    last = low_frequency * growth_ratio ** (NF - 1)
    rows = [
        f,
        f * (2.0 * math.pi / gravity),
        quad_coef * (f / last) ** 2,
        1.0 - np.exp(-ice_rate * (f / last) ** 2),
        low_frequency / f,
    ]
    return np.stack(rows).astype(np.float32)


def direction_table():
    theta = 2.0 * math.pi * np.arange(ND) / ND
    return np.stack([np.cos(theta), np.sin(theta)]).astype(np.float32)


def quad(f, a, b):
    return f * (f * (a * (1 / 2.4414) + b * (1 / 0.3164)) - (a * b) * (2.0 / 0.7725))


def wave_kernel(
    sizes,
    f_hbm, aux_ref, slots_ref, count_ref, table_ref, freq_ref, dir_ref, out_hbm,
    fx, g, ob, rows_out, rows_in, cols_in, aux_all, sums, fld, fric, wind,
    load_sem, halo_send, halo_recv, aux_send, aux_recv, sum_send, sum_recv,
    row_send, row_recv, col_send, col_recv, out_sem,
):
    own, nspec, nrow, ncol, most, total_rows = sizes
    me = lax.axis_index("spec")
    band = lax.axis_index("band")
    sub = lax.axis_index("sub")
    half = ncol // 2
    blk_rows = nrow // nspec
    xpos = (me == 0) | (me == nspec - 1)
    ypos = me < nspec // 2
    nxt, prv = lax.rem(me + 1, nspec), lax.rem(me + nspec - 1, nspec)

    load = pltpu.make_async_copy(
        f_hbm, fx.at[pl.ds(REACH, own), pl.ds(PAD, NF)], load_sem
    )
    load.start()
    barrier = pltpu.get_barrier_semaphore()
    for o in range(1, nspec):
        pl.semaphore_signal(
            barrier, inc=1, device_id={"spec": lax.rem(me + o, nspec)}, device_id_type=MESH
        )
    pl.semaphore_signal(barrier, inc=1, device_id={"band": 1 - band}, device_id_type=MESH)
    pl.semaphore_signal(barrier, inc=1, device_id={"sub": 1 - sub}, device_id_type=MESH)
    zero = jnp.zeros((nrow, ncol), jnp.float32)

    def clear(d, _):
        for m in range(PAD):
            fx[d, m] = zero
            fx[d, PAD + NF + m] = zero
        return 0

    lax.fori_loop(0, own + 2 * REACH, clear, 0)
    pl.semaphore_wait(barrier, nspec + 1)

    lows, highs = [], []
    for k in range(REACH):
        lows.append(
            pltpu.make_async_remote_copy(
                src_ref=f_hbm.at[own - 1 - k],
                dst_ref=fx.at[REACH - 1 - k, pl.ds(PAD, NF)],
                send_sem=halo_send.at[k],
                recv_sem=halo_recv.at[k],
                device_id={"spec": nxt},
                device_id_type=MESH,
            )
        )
        highs.append(
            pltpu.make_async_remote_copy(
                src_ref=f_hbm.at[k],
                dst_ref=fx.at[REACH + own + k, pl.ds(PAD, NF)],
                send_sem=halo_send.at[REACH + k],
                recv_sem=halo_recv.at[REACH + k],
                device_id={"spec": prv},
                device_id_type=MESH,
            )
        )
    for k in range(REACH):
        lows[k].start()
        highs[k].start()

    place = (
        lax.broadcasted_iota(jnp.int32, (blk_rows, ncol), 0) * ncol
        + lax.broadcasted_iota(jnp.int32, (blk_rows, ncol), 1)
    )
    count = count_ref[0]

    def mark(i, flags):
        for j in range(16):
            m = i * 16 + j
            slot = jnp.where(m < count, slots_ref[m], -1)
            flags = jnp.where(place == slot, 1.0, flags)
        return flags

    flags = lax.fori_loop(0, most // 16, mark, jnp.zeros((blk_rows, ncol), jnp.float32))
    n_aux = 4 * blk_rows
    aux_all[me, pl.ds(0, n_aux)] = aux_ref[...]
    for i in range(blk_rows):
        aux_all[me, n_aux + i] = flags[i : i + 1, :]

    def exchange(buffer, send, recv):
        return [
            pltpu.make_async_remote_copy(
                src_ref=buffer.at[me],
                dst_ref=buffer.at[me],
                send_sem=send.at[o - 1],
                recv_sem=recv.at[o - 1],
                device_id={"spec": lax.rem(me + o, nspec)},
                device_id_type=MESH,
            )
            for o in range(1, nspec)
        ]

    def arrivals(buffer, send, recv):
        for o in range(1, nspec):
            pltpu.make_async_remote_copy(
                src_ref=buffer.at[me],
                dst_ref=buffer.at[lax.rem(me + nspec - o, nspec)],
                send_sem=send.at[o - 1],
                recv_sem=recv.at[o - 1],
                device_id={"spec": lax.rem(me + o, nspec)},
                device_id_type=MESH,
            ).wait_recv()

    aux_sends = exchange(aux_all, aux_send, aux_recv)
    for c in aux_sends:
        c.start()

    load.wait()

    def add_up(n, carry):
        energy, inverse = carry
        part = fx[REACH, PAD + n]
        for d in range(1, own):
            part = part + fx[REACH + d, PAD + n]
        return energy + part * freq_ref[0, PAD + n], inverse + part

    energy, inverse = lax.fori_loop(0, NF, add_up, (zero, zero))
    sums[me, 0] = energy
    sums[me, 1] = inverse
    sum_sends = exchange(sums, sum_send, sum_recv)
    for c in sum_sends:
        c.start()

    arrivals(aux_all, aux_send, aux_recv)
    for p in range(nspec):
        for f in range(5):
            for i in range(blk_rows):
                r = p * blk_rows + i
                fld[f, r : r + 1, :] = aux_all[p, f * blk_rows + i]
    depth = fld[3]

    def rub(n, _):
        value = zero
        for c in range(table_ref.shape[0]):
            value = jnp.where(depth == float(c), table_ref[c, n], value)
        fric[n] = value
        return 0

    lax.fori_loop(0, NF, rub, 0)

    arrivals(sums, sum_send, sum_recv)
    energy = sums[0, 0]
    inverse = sums[0, 1]
    for p in range(1, nspec):
        energy = energy + sums[p, 0]
        inverse = inverse + sums[p, 1]
    mean_freq = energy / inverse
    energy = energy * UNIT
    mean_wave = mean_freq * mean_freq * (4.0 * math.pi**2 / gravity)
    steep = energy * mean_wave * mean_wave * (1.0 / steep_ref)
    speed, wdir, ice, sea = fld[0], fld[1], fld[2], fld[4]
    open_water = 1.0 - ice
    row = lax.broadcasted_iota(jnp.int32, (nrow, ncol), 0)
    lane = lax.broadcasted_iota(jnp.int32, (nrow, ncol), 1)
    lat = latitudes((row + band * nrow).astype(jnp.float32), total_rows)
    fld[0] = speed * jnp.cos(wdir)
    fld[1] = speed * jnp.sin(wdir)
    fld[2] = sea * ice
    fld[3] = (dissip_coef * steep * steep / mean_freq) * open_water
    fld[5] = wind_coef * open_water
    fld[6] = courant_limit / jnp.cos(lat)

    def source(d):
        t = me * own + d
        wind[...] = fld[0] * dir_ref[0, t] + fld[1] * dir_ref[1, t]

        def one(n, _):
            for h in range(nrow // 8):
                rs = pl.ds(8 * h, 8)

                def F(dd, m):
                    return fx[REACH + d + dd, PAD + m + n, rs, :]

                c = F(0, 0)
                here = quad(c, F(1, 3), F(-3, -4)) + quad(c, F(-1, 3), F(3, -4))
                down = quad(F(-1, -3), c, F(-4, -7)) + quad(F(1, -3), c, F(4, -7))
                up = quad(F(3, 4), F(4, 7), c) + quad(F(-3, 4), F(-4, 7), c)
                transfer = (
                    here * (-2.0 * freq_ref[2, PAD + n])
                    + down * freq_ref[2, PAD + n - 3]
                    + up * freq_ref[2, PAD + n + 4]
                )
                growth = jnp.maximum(wind[rs, :] * freq_ref[1, PAD + n] - 1.0, 0.0) * fld[5, rs, :]
                rate = growth - fld[3, rs, :] * freq_ref[0, PAD + n] - fric[n, rs, :]
                value = jnp.maximum(c * (1.0 + rate) + transfer, 0.0)
                value = value * (fld[4, rs, :] - fld[2, rs, :] * freq_ref[3, PAD + n])
                g[d, n, rs, :] = value
            rows_out[d, n] = jnp.where(ypos, g[d, n, nrow - 1 : nrow, :], g[d, n, 0:1, :])
            return 0

        lax.fori_loop(0, NF, one, 0)

    def edges(d):
        side = pl.multiple_of(xpos.astype(jnp.int32) * half, half)
        return [
            pltpu.make_async_remote_copy(
                src_ref=rows_out.at[d],
                dst_ref=rows_in.at[d],
                send_sem=row_send.at[d],
                recv_sem=row_recv.at[d],
                device_id={"band": 1 - band},
                device_id_type=MESH,
            ),
            pltpu.make_async_remote_copy(
                src_ref=g.at[d, :, :, pl.ds(side, half)],
                dst_ref=cols_in.at[d],
                send_sem=col_send.at[d],
                recv_sem=col_recv.at[d],
                device_id={"sub": 1 - sub},
                device_id_type=MESH,
            ),
        ]

    bands = lax.axis_size("band")
    inside = jnp.where(ypos, band > 0, band < bands - 1).astype(jnp.float32)

    def advance(d):
        t = me * own + d
        cos_d = jnp.abs(dir_ref[0, t])
        sin_d = jnp.abs(dir_ref[1, t]) * courant_limit

        def one(n, _):
            c = g[d, n]
            e = cols_in[d, n]
            wide = jnp.concatenate([e, e], axis=1)
            west = jnp.where(lane == 0, pltpu.roll(wide, 1, 1), pltpu.roll(c, 1, 1))
            east = jnp.where(
                lane == ncol - 1, pltpu.roll(wide, ncol - 1, 1), pltpu.roll(c, ncol - 1, 1)
            )
            far = rows_in[d, n] * inside
            south = jnp.where(row == 0, far, pltpu.roll(c, 1, 0))
            north = jnp.where(row == nrow - 1, far, pltpu.roll(c, nrow - 1, 0))
            gx = jnp.where(xpos, west, east)
            gy = jnp.where(ypos, south, north)
            ratio = freq_ref[4, PAD + n]
            moved = c - (fld[6] * (ratio * cos_d)) * (c - gx) - (ratio * sin_d) * (c - gy)
            ob[d, n] = moved * fld[4]
            return 0

        lax.fori_loop(0, NF, one, 0)
        copy = pltpu.make_async_copy(ob.at[d], out_hbm.at[d], out_sem.at[d])
        copy.start()
        return copy

    mid = own // 2
    order = [mid]
    for k in range(1, mid + 1):
        order += [mid - k, mid + k]
    pending = None
    started, outs = [], []
    for d in order:
        if d < mid:
            lows[mid - d - 1].wait_recv()
        elif d > mid:
            highs[d - mid - 1].wait_recv()
        source(d)
        now = edges(d)
        for c in now:
            c.start()
        started += now
        if pending is not None:
            for c in pending[1]:
                c.wait_recv()
            outs.append(advance(pending[0]))
        pending = (d, now)
    for c in pending[1]:
        c.wait_recv()
    outs.append(advance(pending[0]))
    for c in started + lows + highs + aux_sends + sum_sends:
        c.wait_send()
    for c in outs:
        c.wait()


def halo_body(spectrum, wind_speed, wind_dir, ice_mask, depth_class, bottom_table, sea_slots, sea_count):
    comps, nrow, ncol = spectrum.shape
    nspec = lax.axis_size("spec")
    own = comps // NF
    most = sea_slots.shape[-1]
    blk_rows = nrow // nspec
    total_rows = nrow * lax.axis_size("band")
    aux = jnp.stack(
        [
            wind_speed.reshape(blk_rows, 1, ncol),
            wind_dir.reshape(blk_rows, 1, ncol),
            ice_mask.reshape(blk_rows, 1, ncol).astype(jnp.float32),
            depth_class.reshape(blk_rows, 1, ncol).astype(jnp.float32),
        ]
    ).reshape(4 * blk_rows, 1, ncol)
    f32 = jnp.float32
    hbm = pl.BlockSpec(memory_space=pl.ANY)
    vmem = pl.BlockSpec(memory_space=pltpu.VMEM)
    smem = pl.BlockSpec(memory_space=pltpu.SMEM)
    dma = pltpu.SemaphoreType.DMA
    moved = pl.pallas_call(
        functools.partial(wave_kernel, (own, nspec, nrow, ncol, most, total_rows)),
        out_shape=jax.ShapeDtypeStruct((own, NF, nrow, ncol), f32),
        in_specs=[hbm, vmem, smem, smem, smem, smem, smem],
        out_specs=hbm,
        scratch_shapes=[
            pltpu.VMEM((own + 2 * REACH, NF + 2 * PAD, nrow, ncol), f32),
            pltpu.VMEM((own, NF, nrow, ncol), f32),
            pltpu.VMEM((own, NF, nrow, ncol), f32),
            pltpu.VMEM((own, NF, 1, ncol), f32),
            pltpu.VMEM((own, NF, 1, ncol), f32),
            pltpu.VMEM((own, NF, nrow, ncol // 2), f32),
            pltpu.VMEM((nspec, 5 * blk_rows, 1, ncol), f32),
            pltpu.VMEM((nspec, 2, nrow, ncol), f32),
            pltpu.VMEM((7, nrow, ncol), f32),
            pltpu.VMEM((NF, nrow, ncol), f32),
            pltpu.VMEM((nrow, ncol), f32),
            dma,
            dma((2 * REACH,)),
            dma((2 * REACH,)),
            dma((nspec - 1,)),
            dma((nspec - 1,)),
            dma((nspec - 1,)),
            dma((nspec - 1,)),
            dma((own,)),
            dma((own,)),
            dma((own,)),
            dma((own,)),
            dma((own,)),
        ],
        compiler_params=pltpu.CompilerParams(
            collective_id=0, has_side_effects=True, vmem_limit_bytes=56 * 2**20
        ),
    )(
        spectrum.reshape(own, NF, nrow, ncol),
        aux,
        sea_slots.reshape(most),
        sea_count.reshape(1),
        bottom_table,
        jnp.asarray(frequency_table()),
        jnp.asarray(direction_table()),
    )
    return moved.reshape(comps, nrow, ncol)


def step(shape, spectrum, *rest):
    comps, nrow, ncol = spectrum.shape
    fits = (
        shape["spec"] == 4
        and comps * 4 == ND * NF
        and shape["band"] == 2
        and shape["sub"] == 2
        and nrow % 8 == 0
        and ncol % 256 == 0
    )
    return (halo_body if fits else body)(spectrum, *rest)


def solution(mesh):
    return jax.shard_map(
        functools.partial(step, dict(mesh.shape)),
        mesh=mesh,
        in_specs=(
            P(("groups", "spec"), "band", "sub"),
            P(("groups", "band"), "sub", "spec", None),
            P(("groups", "band"), "sub", "spec", None),
            P(("groups", "band"), "sub", "spec", None),
            P(("groups", "band"), "sub", "spec", None),
            P(),
            P(("groups", "band"), "sub", "spec", None),
            P(("groups", "band"), "sub", "spec", None),
        ),
        out_specs=P(("groups", "spec"), "band", "sub"),
        check_vma=False,
    )
```

```python
import math

import functools

import jax
import jax.numpy as jnp
import numpy as np
from jax import lax
from jax.experimental import pallas as pl
from jax.experimental.pallas import tpu as pltpu
from jax.sharding import PartitionSpec as P

ND = 36
NF = 48


low_frequency = 0.04
growth_ratio = 1.07
courant_limit = 0.44
gravity = 9.81
wind_coef = 0.02
dissip_coef = 0.03
steep_ref = 0.4
quad_coef = 0.02
ice_rate = 0.5


def with_halo(block, sides, width, periodic):
    for axis, dim in sides:
        count = lax.axis_size(axis)
        forward = [(i, i + 1) for i in range(count - 1)]
        if periodic:
            forward.append((count - 1, 0))
        backward = [(target, source) for source, target in forward]
        low = lax.ppermute(
            lax.slice_in_dim(block, block.shape[dim] - width, None, axis=dim), axis, forward
        )
        high = lax.ppermute(lax.slice_in_dim(block, 0, width, axis=dim), axis, backward)
        block = jnp.concatenate([low, block, high], axis=dim)
    return block


def frequencies(index):
    return low_frequency * jnp.exp(index * math.log(growth_ratio))


def shifted(values, dir_turn, offset):
    rolled = jnp.roll(values, dir_turn, axis=0)
    count_freqs = values.shape[1]
    if offset > 0:
        padding = jnp.zeros((values.shape[0], offset) + values.shape[2:], values.dtype)
        return jnp.concatenate([padding, rolled[:, : count_freqs - offset]], axis=1)
    padding = jnp.zeros((values.shape[0], -offset) + values.shape[2:], values.dtype)
    return jnp.concatenate([rolled[:, -offset:], padding], axis=1)


def source_step(spectrum, wind_speed, wind_dir, ice_flag, depth_class, sea_flag, bottom_table):
    count_dirs, count_freqs = (spectrum.shape[0], spectrum.shape[1])
    frequency = frequencies(jnp.arange(count_freqs, dtype=jnp.float32))
    bin_width = frequency * (growth_ratio - 1.0 / growth_ratio) * 0.5 * (2.0 * math.pi / count_dirs)
    angles = jnp.arange(count_dirs, dtype=jnp.float32) * (2.0 * math.pi / count_dirs)
    energy_sum = jnp.sum(spectrum * bin_width[None, :, None], axis=(0, 1))
    inverse_sum = jnp.sum(spectrum * (bin_width / frequency)[None, :, None], axis=(0, 1))
    mean_freq = energy_sum / inverse_sum
    mean_wave = mean_freq * mean_freq * (4.0 * math.pi**2 / gravity)
    steepness = energy_sum * mean_wave * mean_wave
    ice_float = ice_flag.astype(jnp.float32)
    open_water = 1.0 - ice_float
    inverse_speed = frequency * (2.0 * math.pi / gravity)
    alignment = jnp.cos(angles[:, None] - wind_dir[None, :])
    wind_ratio = wind_speed[None, None, :] * inverse_speed[None, :, None] * alignment[:, None, :]
    wind_growth = wind_coef * jnp.maximum(wind_ratio - 1.0, 0.0) * open_water[None, None, :]
    dissipation = (
        dissip_coef
        * (frequency[:, None] / mean_freq[None, :])
        * (steepness / steep_ref)[None, :] ** 2
        * open_water[None, :]
    )
    one_hot = (
        depth_class[None, :] == jnp.arange(bottom_table.shape[0], dtype=jnp.int32)[:, None]
    ).astype(jnp.float32)
    friction = jnp.dot(bottom_table.T, one_hot, precision=lax.Precision.HIGHEST)
    net_rate = wind_growth - dissipation[None] - friction[None]
    weights = (quad_coef * (frequency / frequency[-1]) ** 2)[None, :, None]
    center_sq = spectrum * spectrum
    plus_one = shifted(spectrum, -1, -3)
    minus_one = shifted(spectrum, 3, 4)
    plus_two = shifted(spectrum, 1, -3)
    minus_two = shifted(spectrum, -3, 4)
    quad_one = weights * (
        center_sq * (plus_one / 2.4414 + minus_one / 0.3164)
        - 2.0 * spectrum * plus_one * minus_one / 0.7725
    )
    quad_two = weights * (
        center_sq * (plus_two / 2.4414 + minus_two / 0.3164)
        - 2.0 * spectrum * plus_two * minus_two / 0.7725
    )
    transfer = (
        -2.0 * (quad_one + quad_two)
        + shifted(quad_one, 1, 3)
        + shifted(quad_one, -3, -4)
        + shifted(quad_two, -1, 3)
        + shifted(quad_two, 3, -4)
    )
    updated = jnp.maximum(spectrum * (1.0 + net_rate) + transfer, 0.0)
    damping = jnp.exp(-ice_rate * (frequency / frequency[-1]) ** 2)
    ice_factor = 1.0 - ice_float[None, :] * (1.0 - damping[:, None])
    return updated * ice_factor[None] * sea_flag[None, None, :]


def courant_numbers(dir_index, freq_index, latitude, count_dirs):
    ratio = low_frequency / frequencies(freq_index)
    angle = dir_index * (2.0 * math.pi / count_dirs)
    courant_x = courant_limit * (ratio * jnp.cos(angle))[:, None] / jnp.cos(latitude)[None, :]
    courant_y = courant_limit * ratio * jnp.sin(angle)
    return (courant_x, courant_y)


def latitudes(row_index, total_rows):
    degrees = -60.0 + 120.0 * (row_index + 0.5) / total_rows
    return degrees * (math.pi / 180.0)


def upwind_step(padded, courant_x, courant_y):
    center = padded[:, 1:-1, 1:-1]
    east = padded[:, 1:-1, 2:]
    west = padded[:, 1:-1, :-2]
    north = padded[:, 2:, 1:-1]
    south = padded[:, :-2, 1:-1]
    east_go = jnp.maximum(courant_x, 0.0)[:, :, None]
    west_go = jnp.minimum(courant_x, 0.0)[:, :, None]
    north_go = jnp.maximum(courant_y, 0.0)[:, None, None]
    south_go = jnp.minimum(courant_y, 0.0)[:, None, None]
    flux_east = east_go * center + west_go * east
    flux_west = east_go * west + west_go * center
    flux_north = north_go * center + south_go * north
    flux_south = north_go * south + south_go * center
    return center - (flux_east - flux_west) - (flux_north - flux_south)


def body(spectrum, wind_speed, wind_dir, ice_mask, depth_class, bottom_table, sea_slots, sea_count):
    local_comps, rows, cols = spectrum.shape
    spec_size = lax.axis_size("spec")
    block_len = rows * cols // spec_size
    most = sea_slots.shape[-1]
    all_slots, all_counts = (
        lax.all_gather(sea_slots, "spec", axis=2, tiled=True),
        lax.all_gather(sea_count, "spec", axis=2, tiled=True),
    )
    all_slots = all_slots.reshape(spec_size, most)
    all_counts = all_counts.reshape(spec_size, 1)
    slot_range = jnp.arange(most, dtype=jnp.int32)
    all_live = (slot_range[None, :] < all_counts).astype(jnp.float32)
    block_rows = jnp.arange(spec_size, dtype=jnp.int32)[:, None]
    sea_prop = (
        jnp.zeros((spec_size, block_len), jnp.float32).at[block_rows, all_slots].set(all_live)
    )
    my_slots = sea_slots.reshape(most)
    my_live = (slot_range < sea_count.reshape(())).astype(jnp.float32)
    speed_row = wind_speed.reshape(block_len)
    dir_row = wind_dir.reshape(block_len)
    ice_row = ice_mask.reshape(block_len)
    depth_row = depth_class.reshape(block_len)
    blocks = spectrum.reshape(local_comps, spec_size, block_len)
    gathered = lax.all_to_all(blocks, "spec", split_axis=1, concat_axis=0, tiled=True)
    sea_own = jnp.zeros((block_len,), jnp.float32).at[my_slots].set(my_live)
    sourced = source_step(
        gathered.reshape(ND, NF, block_len),
        speed_row,
        dir_row,
        ice_row,
        depth_row,
        sea_own,
        bottom_table,
    )
    stepped = lax.all_to_all(
        sourced.reshape(ND * NF, 1, block_len), "spec", split_axis=0, concat_axis=1, tiled=True
    )
    grid_part = stepped.reshape(local_comps, rows, cols)
    with_rows = with_halo(grid_part, (("band", 1),), 1, False)
    padded = with_halo(with_rows, (("sub", 2),), 1, True)
    comp_index = lax.axis_index("spec") * local_comps + jnp.arange(local_comps, dtype=jnp.int32)
    dir_index = (comp_index // NF).astype(jnp.float32)
    freq_index = (comp_index % NF).astype(jnp.float32)
    row_index = (lax.axis_index("band") * rows + jnp.arange(rows, dtype=jnp.int32)).astype(
        jnp.float32
    )
    latitude = latitudes(row_index, rows * lax.axis_size("band"))
    courant_x, courant_y = courant_numbers(dir_index, freq_index, latitude, ND)
    moved = upwind_step(padded, courant_x, courant_y)
    return moved * sea_prop.reshape(rows, cols)[None]


REACH = 4
PAD = 7
MESH = pl.DeviceIdType.MESH
UNIT = (growth_ratio - 1.0 / growth_ratio) * 0.5 * (2.0 * math.pi / ND)


def frequency_table():
    n = np.arange(-PAD, NF + PAD, dtype=np.float64)
    f = low_frequency * growth_ratio**n
    last = low_frequency * growth_ratio ** (NF - 1)
    rows = [
        f,
        f * (2.0 * math.pi / gravity),
        quad_coef * (f / last) ** 2,
        1.0 - np.exp(-ice_rate * (f / last) ** 2),
        low_frequency / f,
    ]
    return np.stack(rows).astype(np.float32)


def direction_table():
    theta = 2.0 * math.pi * np.arange(ND) / ND
    return np.stack([np.cos(theta), np.sin(theta)]).astype(np.float32)


def quad(f, a, b):
    return f * (f * (a * (1 / 2.4414) + b * (1 / 0.3164)) - (a * b) * (2.0 / 0.7725))


def wave_kernel(
    sizes,
    f_hbm, aux_ref, slots_ref, count_ref, table_ref, freq_ref, dir_ref, out_hbm,
    fx, g, ob, rows_out, rows_in, cols_in, aux_all, sums, fld, fric, wind,
    load_sem, halo_send, halo_recv, aux_send, aux_recv, sum_send, sum_recv,
    row_send, row_recv, col_send, col_recv, out_sem,
):
    own, nspec, nrow, ncol, most, total_rows = sizes
    me = lax.axis_index("spec")
    band = lax.axis_index("band")
    sub = lax.axis_index("sub")
    half = ncol // 2
    blk_rows = nrow // nspec
    xpos = (me == 0) | (me == nspec - 1)
    ypos = me < nspec // 2
    nxt, prv = lax.rem(me + 1, nspec), lax.rem(me + nspec - 1, nspec)

    load = pltpu.make_async_copy(
        f_hbm, fx.at[pl.ds(REACH, own), pl.ds(PAD, NF)], load_sem
    )
    load.start()
    barrier = pltpu.get_barrier_semaphore()
    for o in range(1, nspec):
        pl.semaphore_signal(
            barrier, inc=1, device_id={"spec": lax.rem(me + o, nspec)}, device_id_type=MESH
        )
    pl.semaphore_signal(barrier, inc=1, device_id={"band": 1 - band}, device_id_type=MESH)
    pl.semaphore_signal(barrier, inc=1, device_id={"sub": 1 - sub}, device_id_type=MESH)
    zero = jnp.zeros((nrow, ncol), jnp.float32)

    def clear(d, _):
        for m in range(PAD):
            fx[d, m] = zero
            fx[d, PAD + NF + m] = zero
        return 0

    lax.fori_loop(0, own + 2 * REACH, clear, 0)
    pl.semaphore_wait(barrier, nspec + 1)

    lows, highs = [], []
    for k in range(REACH):
        lows.append(
            pltpu.make_async_remote_copy(
                src_ref=f_hbm.at[own - 1 - k],
                dst_ref=fx.at[REACH - 1 - k, pl.ds(PAD, NF)],
                send_sem=halo_send.at[k],
                recv_sem=halo_recv.at[k],
                device_id={"spec": nxt},
                device_id_type=MESH,
            )
        )
        highs.append(
            pltpu.make_async_remote_copy(
                src_ref=f_hbm.at[k],
                dst_ref=fx.at[REACH + own + k, pl.ds(PAD, NF)],
                send_sem=halo_send.at[REACH + k],
                recv_sem=halo_recv.at[REACH + k],
                device_id={"spec": prv},
                device_id_type=MESH,
            )
        )
    lows[0].start()
    highs[0].start()

    place = (
        lax.broadcasted_iota(jnp.int32, (blk_rows, ncol), 0) * ncol
        + lax.broadcasted_iota(jnp.int32, (blk_rows, ncol), 1)
    )
    count = count_ref[0]

    def mark(i, flags):
        for j in range(16):
            m = i * 16 + j
            slot = jnp.where(m < count, slots_ref[m], -1)
            flags = jnp.where(place == slot, 1.0, flags)
        return flags

    flags = lax.fori_loop(0, most // 16, mark, jnp.zeros((blk_rows, ncol), jnp.float32))
    n_aux = 4 * blk_rows
    aux_all[me, pl.ds(0, n_aux)] = aux_ref[...]
    for i in range(blk_rows):
        aux_all[me, n_aux + i] = flags[i : i + 1, :]

    def exchange(buffer, send, recv):
        return [
            pltpu.make_async_remote_copy(
                src_ref=buffer.at[me],
                dst_ref=buffer.at[me],
                send_sem=send.at[o - 1],
                recv_sem=recv.at[o - 1],
                device_id={"spec": lax.rem(me + o, nspec)},
                device_id_type=MESH,
            )
            for o in range(1, nspec)
        ]

    def arrivals(buffer, send, recv):
        for o in range(1, nspec):
            pltpu.make_async_remote_copy(
                src_ref=buffer.at[me],
                dst_ref=buffer.at[lax.rem(me + nspec - o, nspec)],
                send_sem=send.at[o - 1],
                recv_sem=recv.at[o - 1],
                device_id={"spec": lax.rem(me + o, nspec)},
                device_id_type=MESH,
            ).wait_recv()

    aux_sends = exchange(aux_all, aux_send, aux_recv)
    for c in aux_sends:
        c.start()

    load.wait()

    def add_up(n, carry):
        energy, inverse = carry
        part = fx[REACH, PAD + n]
        for d in range(1, own):
            part = part + fx[REACH + d, PAD + n]
        return energy + part * freq_ref[0, PAD + n], inverse + part

    energy, inverse = lax.fori_loop(0, NF, add_up, (zero, zero))
    sums[me, 0] = energy
    sums[me, 1] = inverse
    sum_sends = exchange(sums, sum_send, sum_recv)
    for c in sum_sends:
        c.start()
    lows[1].start()
    highs[1].start()

    arrivals(aux_all, aux_send, aux_recv)
    for p in range(nspec):
        for f in range(5):
            for i in range(blk_rows):
                r = p * blk_rows + i
                fld[f, r : r + 1, :] = aux_all[p, f * blk_rows + i]
    depth = fld[3]

    def rub(n, _):
        value = zero
        for c in range(table_ref.shape[0]):
            value = jnp.where(depth == float(c), table_ref[c, n], value)
        fric[n] = value
        return 0

    lax.fori_loop(0, NF, rub, 0)

    arrivals(sums, sum_send, sum_recv)
    energy = sums[0, 0]
    inverse = sums[0, 1]
    for p in range(1, nspec):
        energy = energy + sums[p, 0]
        inverse = inverse + sums[p, 1]
    mean_freq = energy / inverse
    energy = energy * UNIT
    mean_wave = mean_freq * mean_freq * (4.0 * math.pi**2 / gravity)
    steep = energy * mean_wave * mean_wave * (1.0 / steep_ref)
    speed, wdir, ice, sea = fld[0], fld[1], fld[2], fld[4]
    open_water = 1.0 - ice
    row = lax.broadcasted_iota(jnp.int32, (nrow, ncol), 0)
    lat = latitudes((row + band * nrow).astype(jnp.float32), total_rows)
    fld[0] = speed * jnp.cos(wdir)
    fld[1] = speed * jnp.sin(wdir)
    fld[2] = sea * ice
    fld[3] = (dissip_coef * steep * steep / mean_freq) * open_water
    fld[5] = wind_coef * open_water
    fld[6] = courant_limit / jnp.cos(lat)

    def source(d):
        t = me * own + d
        wind[...] = fld[0] * dir_ref[0, t] + fld[1] * dir_ref[1, t]

        def one(n, _):
            for h in range(nrow // 8):
                rs = pl.ds(8 * h, 8)

                def F(dd, m):
                    return fx[REACH + d + dd, PAD + m + n, rs, :]

                c = F(0, 0)
                here = quad(c, F(1, 3), F(-3, -4)) + quad(c, F(-1, 3), F(3, -4))
                down = quad(F(-1, -3), c, F(-4, -7)) + quad(F(1, -3), c, F(4, -7))
                up = quad(F(3, 4), F(4, 7), c) + quad(F(-3, 4), F(-4, 7), c)
                transfer = (
                    here * (-2.0 * freq_ref[2, PAD + n])
                    + down * freq_ref[2, PAD + n - 3]
                    + up * freq_ref[2, PAD + n + 4]
                )
                growth = jnp.maximum(wind[rs, :] * freq_ref[1, PAD + n] - 1.0, 0.0) * fld[5, rs, :]
                rate = growth - fld[3, rs, :] * freq_ref[0, PAD + n] - fric[n, rs, :]
                value = jnp.maximum(c * (1.0 + rate) + transfer, 0.0)
                value = value * (fld[4, rs, :] - fld[2, rs, :] * freq_ref[3, PAD + n])
                g[d, n, rs, :] = value
            rows_out[d, n] = jnp.where(ypos, g[d, n, nrow - 1 : nrow, :], g[d, n, 0:1, :])
            return 0

        lax.fori_loop(0, NF, one, 0)

    def edges(d):
        side = pl.multiple_of(xpos.astype(jnp.int32) * half, half)
        return [
            pltpu.make_async_remote_copy(
                src_ref=rows_out.at[d],
                dst_ref=rows_in.at[d],
                send_sem=row_send.at[d],
                recv_sem=row_recv.at[d],
                device_id={"band": 1 - band},
                device_id_type=MESH,
            ),
            pltpu.make_async_remote_copy(
                src_ref=g.at[d, :, :, pl.ds(side, half)],
                dst_ref=cols_in.at[d],
                send_sem=col_send.at[d],
                recv_sem=col_recv.at[d],
                device_id={"sub": 1 - sub},
                device_id_type=MESH,
            ),
        ]

    bands = lax.axis_size("band")
    inside = jnp.where(ypos, band > 0, band < bands - 1).astype(jnp.float32)

    xshift = jnp.where(xpos, 1, half - 1)
    yshift = jnp.where(ypos, 1, 7)
    nt = nrow // 8
    lane = lax.broadcasted_iota(jnp.int32, (nrow, half), 1)
    tier = lax.broadcasted_iota(jnp.int32, (8, ncol), 0)
    xlow = lane == jnp.where(xpos, 0, -1)
    xhigh = lane == jnp.where(xpos, -1, half - 1)
    ylow = tier == jnp.where(ypos, 0, -1)
    yhigh = tier == jnp.where(ypos, -1, 7)

    def advance(d):
        t = me * own + d
        cos_d = jnp.abs(dir_ref[0, t])
        sin_d = jnp.abs(dir_ref[1, t]) * courant_limit

        def one(i, _):
            for j in range(4):
                n = i * 4 + j
                c = g[d, n]
                e = pltpu.roll(cols_in[d, n], xshift, 1)
                r0 = pltpu.roll(c[:, :half], xshift, 1)
                r1 = pltpu.roll(c[:, half:], xshift, 1)
                gx = jnp.concatenate(
                    [
                        jnp.where(xlow, e, jnp.where(xhigh, r1, r0)),
                        jnp.where(xhigh, e, jnp.where(xlow, r0, r1)),
                    ],
                    axis=1,
                )
                far = rows_in[d, n] * inside
                tiles = [pltpu.roll(c[8 * k : 8 * k + 8], yshift, 0) for k in range(nt)]
                parts = []
                for k in range(nt):
                    below = tiles[k - 1] if k > 0 else far
                    above = tiles[k + 1] if k < nt - 1 else far
                    parts.append(jnp.where(ylow, below, jnp.where(yhigh, above, tiles[k])))
                gy = jnp.concatenate(parts, axis=0)
                ratio = freq_ref[4, PAD + n]
                moved = c - (fld[6] * (ratio * cos_d)) * (c - gx) - (ratio * sin_d) * (c - gy)
                ob[d, n] = moved * fld[4]
            return 0

        lax.fori_loop(0, NF // 4, one, 0)
        copy = pltpu.make_async_copy(ob.at[d], out_hbm.at[d], out_sem.at[d])
        copy.start()
        return copy

    mid = own // 2
    order = [mid]
    for k in range(1, mid + 1):
        order += [mid - k, mid + k]
    pending = None
    started, outs = [], []
    for d in order:
        if d < mid:
            k = mid - d - 1
            lows[k].wait_recv()
            for side in (lows, highs):
                side[k].wait_send()
                if k + 2 < REACH:
                    side[k + 2].start()
        elif d > mid:
            highs[d - mid - 1].wait_recv()
        source(d)
        now = edges(d)
        for c in now:
            c.start()
        started += now
        if pending is not None:
            for c in pending[1]:
                c.wait_recv()
            outs.append(advance(pending[0]))
        pending = (d, now)
    for c in pending[1]:
        c.wait_recv()
    outs.append(advance(pending[0]))
    for c in started + aux_sends + sum_sends:
        c.wait_send()
    for c in outs:
        c.wait()


def halo_body(spectrum, wind_speed, wind_dir, ice_mask, depth_class, bottom_table, sea_slots, sea_count):
    comps, nrow, ncol = spectrum.shape
    nspec = lax.axis_size("spec")
    own = comps // NF
    most = sea_slots.shape[-1]
    blk_rows = nrow // nspec
    total_rows = nrow * lax.axis_size("band")
    aux = jnp.stack(
        [
            wind_speed.reshape(blk_rows, 1, ncol),
            wind_dir.reshape(blk_rows, 1, ncol),
            ice_mask.reshape(blk_rows, 1, ncol).astype(jnp.float32),
            depth_class.reshape(blk_rows, 1, ncol).astype(jnp.float32),
        ]
    ).reshape(4 * blk_rows, 1, ncol)
    f32 = jnp.float32
    hbm = pl.BlockSpec(memory_space=pl.ANY)
    vmem = pl.BlockSpec(memory_space=pltpu.VMEM)
    smem = pl.BlockSpec(memory_space=pltpu.SMEM)
    dma = pltpu.SemaphoreType.DMA
    moved = pl.pallas_call(
        functools.partial(wave_kernel, (own, nspec, nrow, ncol, most, total_rows)),
        out_shape=jax.ShapeDtypeStruct((own, NF, nrow, ncol), f32),
        in_specs=[hbm, vmem, smem, smem, smem, smem, smem],
        out_specs=hbm,
        scratch_shapes=[
            pltpu.VMEM((own + 2 * REACH, NF + 2 * PAD, nrow, ncol), f32),
            pltpu.VMEM((own, NF, nrow, ncol), f32),
            pltpu.VMEM((own, NF, nrow, ncol), f32),
            pltpu.VMEM((own, NF, 1, ncol), f32),
            pltpu.VMEM((own, NF, 1, ncol), f32),
            pltpu.VMEM((own, NF, nrow, ncol // 2), f32),
            pltpu.VMEM((nspec, 5 * blk_rows, 1, ncol), f32),
            pltpu.VMEM((nspec, 2, nrow, ncol), f32),
            pltpu.VMEM((7, nrow, ncol), f32),
            pltpu.VMEM((NF, nrow, ncol), f32),
            pltpu.VMEM((nrow, ncol), f32),
            dma,
            dma((2 * REACH,)),
            dma((2 * REACH,)),
            dma((nspec - 1,)),
            dma((nspec - 1,)),
            dma((nspec - 1,)),
            dma((nspec - 1,)),
            dma((own,)),
            dma((own,)),
            dma((own,)),
            dma((own,)),
            dma((own,)),
        ],
        compiler_params=pltpu.CompilerParams(
            collective_id=0, has_side_effects=True, vmem_limit_bytes=56 * 2**20
        ),
    )(
        spectrum.reshape(own, NF, nrow, ncol),
        aux,
        sea_slots.reshape(most),
        sea_count.reshape(1),
        bottom_table,
        jnp.asarray(frequency_table()),
        jnp.asarray(direction_table()),
    )
    return moved.reshape(comps, nrow, ncol)


def step(shape, spectrum, *rest):
    comps, nrow, ncol = spectrum.shape
    fits = (
        shape["spec"] == 4
        and comps * 4 == ND * NF
        and shape["band"] == 2
        and shape["sub"] == 2
        and nrow % 8 == 0
        and ncol % 256 == 0
    )
    return (halo_body if fits else body)(spectrum, *rest)


def solution(mesh):
    return jax.shard_map(
        functools.partial(step, dict(mesh.shape)),
        mesh=mesh,
        in_specs=(
            P(("groups", "spec"), "band", "sub"),
            P(("groups", "band"), "sub", "spec", None),
            P(("groups", "band"), "sub", "spec", None),
            P(("groups", "band"), "sub", "spec", None),
            P(("groups", "band"), "sub", "spec", None),
            P(),
            P(("groups", "band"), "sub", "spec", None),
            P(("groups", "band"), "sub", "spec", None),
        ),
        out_specs=P(("groups", "spec"), "band", "sub"),
        check_vma=False,
    )
```

```python
import math

import functools

import jax
import jax.numpy as jnp
import numpy as np
from jax import lax
from jax.experimental import pallas as pl
from jax.experimental.pallas import tpu as pltpu
from jax.sharding import PartitionSpec as P

ND = 36
NF = 48


low_frequency = 0.04
growth_ratio = 1.07
courant_limit = 0.44
gravity = 9.81
wind_coef = 0.02
dissip_coef = 0.03
steep_ref = 0.4
quad_coef = 0.02
ice_rate = 0.5


def with_halo(block, sides, width, periodic):
    for axis, dim in sides:
        count = lax.axis_size(axis)
        forward = [(i, i + 1) for i in range(count - 1)]
        if periodic:
            forward.append((count - 1, 0))
        backward = [(target, source) for source, target in forward]
        low = lax.ppermute(
            lax.slice_in_dim(block, block.shape[dim] - width, None, axis=dim), axis, forward
        )
        high = lax.ppermute(lax.slice_in_dim(block, 0, width, axis=dim), axis, backward)
        block = jnp.concatenate([low, block, high], axis=dim)
    return block


def frequencies(index):
    return low_frequency * jnp.exp(index * math.log(growth_ratio))


def shifted(values, dir_turn, offset):
    rolled = jnp.roll(values, dir_turn, axis=0)
    count_freqs = values.shape[1]
    if offset > 0:
        padding = jnp.zeros((values.shape[0], offset) + values.shape[2:], values.dtype)
        return jnp.concatenate([padding, rolled[:, : count_freqs - offset]], axis=1)
    padding = jnp.zeros((values.shape[0], -offset) + values.shape[2:], values.dtype)
    return jnp.concatenate([rolled[:, -offset:], padding], axis=1)


def source_step(spectrum, wind_speed, wind_dir, ice_flag, depth_class, sea_flag, bottom_table):
    count_dirs, count_freqs = (spectrum.shape[0], spectrum.shape[1])
    frequency = frequencies(jnp.arange(count_freqs, dtype=jnp.float32))
    bin_width = frequency * (growth_ratio - 1.0 / growth_ratio) * 0.5 * (2.0 * math.pi / count_dirs)
    angles = jnp.arange(count_dirs, dtype=jnp.float32) * (2.0 * math.pi / count_dirs)
    energy_sum = jnp.sum(spectrum * bin_width[None, :, None], axis=(0, 1))
    inverse_sum = jnp.sum(spectrum * (bin_width / frequency)[None, :, None], axis=(0, 1))
    mean_freq = energy_sum / inverse_sum
    mean_wave = mean_freq * mean_freq * (4.0 * math.pi**2 / gravity)
    steepness = energy_sum * mean_wave * mean_wave
    ice_float = ice_flag.astype(jnp.float32)
    open_water = 1.0 - ice_float
    inverse_speed = frequency * (2.0 * math.pi / gravity)
    alignment = jnp.cos(angles[:, None] - wind_dir[None, :])
    wind_ratio = wind_speed[None, None, :] * inverse_speed[None, :, None] * alignment[:, None, :]
    wind_growth = wind_coef * jnp.maximum(wind_ratio - 1.0, 0.0) * open_water[None, None, :]
    dissipation = (
        dissip_coef
        * (frequency[:, None] / mean_freq[None, :])
        * (steepness / steep_ref)[None, :] ** 2
        * open_water[None, :]
    )
    one_hot = (
        depth_class[None, :] == jnp.arange(bottom_table.shape[0], dtype=jnp.int32)[:, None]
    ).astype(jnp.float32)
    friction = jnp.dot(bottom_table.T, one_hot, precision=lax.Precision.HIGHEST)
    net_rate = wind_growth - dissipation[None] - friction[None]
    weights = (quad_coef * (frequency / frequency[-1]) ** 2)[None, :, None]
    center_sq = spectrum * spectrum
    plus_one = shifted(spectrum, -1, -3)
    minus_one = shifted(spectrum, 3, 4)
    plus_two = shifted(spectrum, 1, -3)
    minus_two = shifted(spectrum, -3, 4)
    quad_one = weights * (
        center_sq * (plus_one / 2.4414 + minus_one / 0.3164)
        - 2.0 * spectrum * plus_one * minus_one / 0.7725
    )
    quad_two = weights * (
        center_sq * (plus_two / 2.4414 + minus_two / 0.3164)
        - 2.0 * spectrum * plus_two * minus_two / 0.7725
    )
    transfer = (
        -2.0 * (quad_one + quad_two)
        + shifted(quad_one, 1, 3)
        + shifted(quad_one, -3, -4)
        + shifted(quad_two, -1, 3)
        + shifted(quad_two, 3, -4)
    )
    updated = jnp.maximum(spectrum * (1.0 + net_rate) + transfer, 0.0)
    damping = jnp.exp(-ice_rate * (frequency / frequency[-1]) ** 2)
    ice_factor = 1.0 - ice_float[None, :] * (1.0 - damping[:, None])
    return updated * ice_factor[None] * sea_flag[None, None, :]


def courant_numbers(dir_index, freq_index, latitude, count_dirs):
    ratio = low_frequency / frequencies(freq_index)
    angle = dir_index * (2.0 * math.pi / count_dirs)
    courant_x = courant_limit * (ratio * jnp.cos(angle))[:, None] / jnp.cos(latitude)[None, :]
    courant_y = courant_limit * ratio * jnp.sin(angle)
    return (courant_x, courant_y)


def latitudes(row_index, total_rows):
    degrees = -60.0 + 120.0 * (row_index + 0.5) / total_rows
    return degrees * (math.pi / 180.0)


def upwind_step(padded, courant_x, courant_y):
    center = padded[:, 1:-1, 1:-1]
    east = padded[:, 1:-1, 2:]
    west = padded[:, 1:-1, :-2]
    north = padded[:, 2:, 1:-1]
    south = padded[:, :-2, 1:-1]
    east_go = jnp.maximum(courant_x, 0.0)[:, :, None]
    west_go = jnp.minimum(courant_x, 0.0)[:, :, None]
    north_go = jnp.maximum(courant_y, 0.0)[:, None, None]
    south_go = jnp.minimum(courant_y, 0.0)[:, None, None]
    flux_east = east_go * center + west_go * east
    flux_west = east_go * west + west_go * center
    flux_north = north_go * center + south_go * north
    flux_south = north_go * south + south_go * center
    return center - (flux_east - flux_west) - (flux_north - flux_south)


def body(spectrum, wind_speed, wind_dir, ice_mask, depth_class, bottom_table, sea_slots, sea_count):
    local_comps, rows, cols = spectrum.shape
    spec_size = lax.axis_size("spec")
    block_len = rows * cols // spec_size
    most = sea_slots.shape[-1]
    all_slots, all_counts = (
        lax.all_gather(sea_slots, "spec", axis=2, tiled=True),
        lax.all_gather(sea_count, "spec", axis=2, tiled=True),
    )
    all_slots = all_slots.reshape(spec_size, most)
    all_counts = all_counts.reshape(spec_size, 1)
    slot_range = jnp.arange(most, dtype=jnp.int32)
    all_live = (slot_range[None, :] < all_counts).astype(jnp.float32)
    block_rows = jnp.arange(spec_size, dtype=jnp.int32)[:, None]
    sea_prop = (
        jnp.zeros((spec_size, block_len), jnp.float32).at[block_rows, all_slots].set(all_live)
    )
    my_slots = sea_slots.reshape(most)
    my_live = (slot_range < sea_count.reshape(())).astype(jnp.float32)
    speed_row = wind_speed.reshape(block_len)
    dir_row = wind_dir.reshape(block_len)
    ice_row = ice_mask.reshape(block_len)
    depth_row = depth_class.reshape(block_len)
    blocks = spectrum.reshape(local_comps, spec_size, block_len)
    gathered = lax.all_to_all(blocks, "spec", split_axis=1, concat_axis=0, tiled=True)
    sea_own = jnp.zeros((block_len,), jnp.float32).at[my_slots].set(my_live)
    sourced = source_step(
        gathered.reshape(ND, NF, block_len),
        speed_row,
        dir_row,
        ice_row,
        depth_row,
        sea_own,
        bottom_table,
    )
    stepped = lax.all_to_all(
        sourced.reshape(ND * NF, 1, block_len), "spec", split_axis=0, concat_axis=1, tiled=True
    )
    grid_part = stepped.reshape(local_comps, rows, cols)
    with_rows = with_halo(grid_part, (("band", 1),), 1, False)
    padded = with_halo(with_rows, (("sub", 2),), 1, True)
    comp_index = lax.axis_index("spec") * local_comps + jnp.arange(local_comps, dtype=jnp.int32)
    dir_index = (comp_index // NF).astype(jnp.float32)
    freq_index = (comp_index % NF).astype(jnp.float32)
    row_index = (lax.axis_index("band") * rows + jnp.arange(rows, dtype=jnp.int32)).astype(
        jnp.float32
    )
    latitude = latitudes(row_index, rows * lax.axis_size("band"))
    courant_x, courant_y = courant_numbers(dir_index, freq_index, latitude, ND)
    moved = upwind_step(padded, courant_x, courant_y)
    return moved * sea_prop.reshape(rows, cols)[None]


REACH = 4
PIECES = 4
DEPTH = 2
PAD = 7
MESH = pl.DeviceIdType.MESH
UNIT = (growth_ratio - 1.0 / growth_ratio) * 0.5 * (2.0 * math.pi / ND)


def frequency_table():
    n = np.arange(-PAD, NF + PAD, dtype=np.float64)
    f = low_frequency * growth_ratio**n
    last = low_frequency * growth_ratio ** (NF - 1)
    rows = [
        f,
        f * (2.0 * math.pi / gravity),
        quad_coef * (f / last) ** 2,
        1.0 - np.exp(-ice_rate * (f / last) ** 2),
        low_frequency / f,
    ]
    return np.stack(rows).astype(np.float32)


def direction_table():
    theta = 2.0 * math.pi * np.arange(ND) / ND
    return np.stack([np.cos(theta), np.sin(theta)]).astype(np.float32)


def quad(f, a, b):
    return f * (f * (a * (1 / 2.4414) + b * (1 / 0.3164)) - (a * b) * (2.0 / 0.7725))


def wave_kernel(
    sizes,
    f_hbm, speed_in, dir_in, ice_in, depth_in, slots_in, count_in, table_in, freq_in, dir_tab, out_hbm,
    speed_ref, dir_in_ref, ice_ref, depth_ref, slots_ref, count_ref, table_ref, freq_ref, dir_ref, small_sem,
    fx, g, ob, rows_out, rows_in, cols_in, aux_all, sums, fld, fric, wind,
    load_sem, halo_send, halo_recv, aux_send, aux_recv, sum_send, sum_recv,
    row_send, row_recv, col_send, col_recv, out_sem,
):
    own, nspec, nrow, ncol, most, total_rows = sizes
    me = lax.axis_index("spec")
    band = lax.axis_index("band")
    sub = lax.axis_index("sub")
    half = ncol // 2
    blk_rows = nrow // nspec
    xpos = (me == 0) | (me == nspec - 1)
    ypos = me < nspec // 2
    nxt, prv = lax.rem(me + 1, nspec), lax.rem(me + nspec - 1, nspec)

    load = pltpu.make_async_copy(
        f_hbm, fx.at[pl.ds(REACH, own), pl.ds(PAD, NF)], load_sem
    )
    load.start()
    smalls = [
        pltpu.make_async_copy(src, dst, small_sem.at[i])
        for i, (src, dst) in enumerate(
            (
                (slots_in, slots_ref),
                (count_in, count_ref),
                (speed_in, speed_ref),
                (dir_in, dir_in_ref),
                (ice_in, ice_ref),
                (depth_in, depth_ref),
                (freq_in, freq_ref),
                (table_in, table_ref),
                (dir_tab, dir_ref),
            )
        )
    ]
    for c in smalls:
        c.start()
    barrier = pltpu.get_barrier_semaphore()
    for o in range(1, nspec):
        pl.semaphore_signal(
            barrier, inc=1, device_id={"spec": lax.rem(me + o, nspec)}, device_id_type=MESH
        )
    pl.semaphore_signal(barrier, inc=1, device_id={"band": 1 - band}, device_id_type=MESH)
    pl.semaphore_signal(barrier, inc=1, device_id={"sub": 1 - sub}, device_id_type=MESH)
    zero = jnp.zeros((nrow, ncol), jnp.float32)

    def clear(d, _):
        for m in range(PAD):
            fx[d, m] = zero
            fx[d, PAD + NF + m] = zero
        return 0

    lax.fori_loop(0, own + 2 * REACH, clear, 0)
    pl.semaphore_wait(barrier, nspec + 1)

    part = NF // PIECES
    lows, highs = [], []
    for k in range(REACH):
        for q in range(PIECES):
            at = k * PIECES + q
            src, dst = pl.ds(q * part, part), pl.ds(PAD + q * part, part)
            lows.append(
                pltpu.make_async_remote_copy(
                    src_ref=f_hbm.at[own - 1 - k, src],
                    dst_ref=fx.at[REACH - 1 - k, dst],
                    send_sem=halo_send.at[at],
                    recv_sem=halo_recv.at[at],
                    device_id={"spec": nxt},
                    device_id_type=MESH,
                )
            )
            highs.append(
                pltpu.make_async_remote_copy(
                    src_ref=f_hbm.at[k, src],
                    dst_ref=fx.at[REACH + own + k, dst],
                    send_sem=halo_send.at[REACH * PIECES + at],
                    recv_sem=halo_recv.at[REACH * PIECES + at],
                    device_id={"spec": prv},
                    device_id_type=MESH,
                )
            )
    for at in range(DEPTH):
        lows[at].start()
        highs[at].start()

    for c in smalls:
        c.wait()

    place = (
        lax.broadcasted_iota(jnp.int32, (blk_rows, ncol), 0) * ncol
        + lax.broadcasted_iota(jnp.int32, (blk_rows, ncol), 1)
    )
    count = count_ref[0, 0, 0, 0]

    def mark(i, flags):
        for j in range(16):
            m = i * 16 + j
            slot = jnp.where(m < count, slots_ref[0, 0, 0, m], -1)
            flags = jnp.where(place == slot, 1.0, flags)
        return flags

    flags = lax.fori_loop(0, most // 16, mark, jnp.zeros((blk_rows, ncol), jnp.float32))
    n_aux = 4 * blk_rows
    for i in range(blk_rows):
        for f, ref in enumerate((speed_ref, dir_in_ref, ice_ref, depth_ref)):
            piece = ref[0, 0, 0:1, i * ncol : (i + 1) * ncol]
            aux_all[me, f * blk_rows + i] = piece.astype(jnp.float32)
        aux_all[me, n_aux + i] = flags[i : i + 1, :]

    def exchange(buffer, send, recv):
        return [
            pltpu.make_async_remote_copy(
                src_ref=buffer.at[me],
                dst_ref=buffer.at[me],
                send_sem=send.at[o - 1],
                recv_sem=recv.at[o - 1],
                device_id={"spec": lax.rem(me + o, nspec)},
                device_id_type=MESH,
            )
            for o in range(1, nspec)
        ]

    def arrivals(buffer, send, recv):
        for o in range(1, nspec):
            pltpu.make_async_remote_copy(
                src_ref=buffer.at[me],
                dst_ref=buffer.at[lax.rem(me + nspec - o, nspec)],
                send_sem=send.at[o - 1],
                recv_sem=recv.at[o - 1],
                device_id={"spec": lax.rem(me + o, nspec)},
                device_id_type=MESH,
            ).wait_recv()

    aux_sends = exchange(aux_all, aux_send, aux_recv)
    for c in aux_sends:
        c.start()

    load.wait()

    def add_up(n, carry):
        energy, inverse = carry
        part = fx[REACH, PAD + n]
        for d in range(1, own):
            part = part + fx[REACH + d, PAD + n]
        return energy + part * freq_ref[0, PAD + n], inverse + part

    energy, inverse = lax.fori_loop(0, NF, add_up, (zero, zero))
    sums[me, 0] = energy
    sums[me, 1] = inverse
    sum_sends = exchange(sums, sum_send, sum_recv)
    for c in sum_sends:
        c.start()

    arrivals(aux_all, aux_send, aux_recv)
    for p in range(nspec):
        for f in range(5):
            for i in range(blk_rows):
                r = p * blk_rows + i
                fld[f, r : r + 1, :] = aux_all[p, f * blk_rows + i]
    depth = fld[3]

    def rub(n, _):
        value = zero
        for c in range(table_ref.shape[0]):
            value = jnp.where(depth == float(c), table_ref[c, n], value)
        fric[n] = value
        return 0

    lax.fori_loop(0, NF, rub, 0)

    arrivals(sums, sum_send, sum_recv)
    energy = sums[0, 0]
    inverse = sums[0, 1]
    for p in range(1, nspec):
        energy = energy + sums[p, 0]
        inverse = inverse + sums[p, 1]
    mean_freq = energy / inverse
    energy = energy * UNIT
    mean_wave = mean_freq * mean_freq * (4.0 * math.pi**2 / gravity)
    steep = energy * mean_wave * mean_wave * (1.0 / steep_ref)
    speed, wdir, ice, sea = fld[0], fld[1], fld[2], fld[4]
    open_water = 1.0 - ice
    row = lax.broadcasted_iota(jnp.int32, (nrow, ncol), 0)
    lat = latitudes((row + band * nrow).astype(jnp.float32), total_rows)
    fld[0] = speed * jnp.cos(wdir)
    fld[1] = speed * jnp.sin(wdir)
    fld[2] = sea * ice
    fld[3] = (dissip_coef * steep * steep / mean_freq) * open_water
    fld[5] = wind_coef * open_water
    fld[6] = courant_limit / jnp.cos(lat)

    def source(d, first, end):
        t = me * own + d
        wind[...] = fld[0] * dir_ref[0, t] + fld[1] * dir_ref[1, t]

        def one(n, _):
            for h in range(nrow // 8):
                rs = pl.ds(8 * h, 8)

                def F(dd, m):
                    return fx[REACH + d + dd, PAD + m + n, rs, :]

                c = F(0, 0)
                here = quad(c, F(1, 3), F(-3, -4)) + quad(c, F(-1, 3), F(3, -4))
                down = quad(F(-1, -3), c, F(-4, -7)) + quad(F(1, -3), c, F(4, -7))
                up = quad(F(3, 4), F(4, 7), c) + quad(F(-3, 4), F(-4, 7), c)
                transfer = (
                    here * (-2.0 * freq_ref[2, PAD + n])
                    + down * freq_ref[2, PAD + n - 3]
                    + up * freq_ref[2, PAD + n + 4]
                )
                growth = jnp.maximum(wind[rs, :] * freq_ref[1, PAD + n] - 1.0, 0.0) * fld[5, rs, :]
                rate = growth - fld[3, rs, :] * freq_ref[0, PAD + n] - fric[n, rs, :]
                value = jnp.maximum(c * (1.0 + rate) + transfer, 0.0)
                value = value * (fld[4, rs, :] - fld[2, rs, :] * freq_ref[3, PAD + n])
                g[d, n, rs, :] = value
            rows_out[d, n] = jnp.where(ypos, g[d, n, nrow - 1 : nrow, :], g[d, n, 0:1, :])
            return 0

        lax.fori_loop(first, end, one, 0)

    def edges(d):
        side = pl.multiple_of(xpos.astype(jnp.int32) * half, half)
        return [
            pltpu.make_async_remote_copy(
                src_ref=rows_out.at[d],
                dst_ref=rows_in.at[d],
                send_sem=row_send.at[d],
                recv_sem=row_recv.at[d],
                device_id={"band": 1 - band},
                device_id_type=MESH,
            ),
            pltpu.make_async_remote_copy(
                src_ref=g.at[d, :, :, pl.ds(side, half)],
                dst_ref=cols_in.at[d],
                send_sem=col_send.at[d],
                recv_sem=col_recv.at[d],
                device_id={"sub": 1 - sub},
                device_id_type=MESH,
            ),
        ]

    bands = lax.axis_size("band")
    inside = jnp.where(ypos, band > 0, band < bands - 1).astype(jnp.float32)

    xshift = jnp.where(xpos, 1, half - 1)
    yshift = jnp.where(ypos, 1, 7)
    nt = nrow // 8
    lane = lax.broadcasted_iota(jnp.int32, (nrow, half), 1)
    tier = lax.broadcasted_iota(jnp.int32, (8, ncol), 0)
    xlow = lane == jnp.where(xpos, 0, -1)
    xhigh = lane == jnp.where(xpos, -1, half - 1)
    ylow = tier == jnp.where(ypos, 0, -1)
    yhigh = tier == jnp.where(ypos, -1, 7)

    def advance(d):
        t = me * own + d
        cos_d = jnp.abs(dir_ref[0, t])
        sin_d = jnp.abs(dir_ref[1, t]) * courant_limit

        def one(i, _):
            for j in range(4):
                n = i * 4 + j
                c = g[d, n]
                e = pltpu.roll(cols_in[d, n], xshift, 1)
                r0 = pltpu.roll(c[:, :half], xshift, 1)
                r1 = pltpu.roll(c[:, half:], xshift, 1)
                gx = jnp.concatenate(
                    [
                        jnp.where(xlow, e, jnp.where(xhigh, r1, r0)),
                        jnp.where(xhigh, e, jnp.where(xlow, r0, r1)),
                    ],
                    axis=1,
                )
                far = rows_in[d, n] * inside
                tiles = [pltpu.roll(c[8 * k : 8 * k + 8], yshift, 0) for k in range(nt)]
                parts = []
                for k in range(nt):
                    below = tiles[k - 1] if k > 0 else far
                    above = tiles[k + 1] if k < nt - 1 else far
                    parts.append(jnp.where(ylow, below, jnp.where(yhigh, above, tiles[k])))
                gy = jnp.concatenate(parts, axis=0)
                ratio = freq_ref[4, PAD + n]
                moved = c - (fld[6] * (ratio * cos_d)) * (c - gx) - (ratio * sin_d) * (c - gy)
                ob[d, n] = moved * fld[4]
            return 0

        lax.fori_loop(0, NF // 4, one, 0)
        copy = pltpu.make_async_copy(ob.at[d], out_hbm.at[d], out_sem.at[d])
        copy.start()
        return copy

    mid = own // 2
    order = [mid]
    for k in range(1, mid + 1):
        order += [mid - k, mid + k]
    pending = None
    final = REACH * PIECES - 1
    cut = NF - part - PAD
    started, outs = [], []
    for d in order:
        first = 0
        if d < mid:
            for at in range((mid - d - 1) * PIECES, (mid - d) * PIECES):
                if at == final:
                    for b in range(final + 1 - PIECES, final):
                        highs[b].wait_recv()
                    source(0, 0, cut)
                    source(own - 1, 0, cut)
                    first = cut
                lows[at].wait_recv()
                for side in (lows, highs):
                    side[at].wait_send()
                    if at + DEPTH < REACH * PIECES:
                        side[at + DEPTH].start()
        elif d > mid:
            for at in range((d - mid - 1) * PIECES, (d - mid) * PIECES):
                if d < own - 1 or at == final:
                    highs[at].wait_recv()
            first = cut if d == own - 1 else 0
        source(d, first, NF)
        now = edges(d)
        for c in now:
            c.start()
        started += now
        if pending is not None:
            for c in pending[1]:
                c.wait_recv()
            outs.append(advance(pending[0]))
        pending = (d, now)
    for c in pending[1]:
        c.wait_recv()
    outs.append(advance(pending[0]))
    for c in started + aux_sends + sum_sends:
        c.wait_send()
    for c in outs:
        c.wait()


def halo_body(spectrum, wind_speed, wind_dir, ice_mask, depth_class, bottom_table, sea_slots, sea_count):
    comps, nrow, ncol = spectrum.shape
    nspec = lax.axis_size("spec")
    own = comps // NF
    most = sea_slots.shape[-1]
    blk_rows = nrow // nspec
    total_rows = nrow * lax.axis_size("band")
    f32 = jnp.float32
    hbm = pl.BlockSpec(memory_space=pl.ANY)
    dma = pltpu.SemaphoreType.DMA
    moved = pl.pallas_call(
        functools.partial(wave_kernel, (own, nspec, nrow, ncol, most, total_rows)),
        out_shape=jax.ShapeDtypeStruct((own, NF, nrow, ncol), f32),
        in_specs=[hbm] * 10,
        out_specs=hbm,
        scratch_shapes=[
            pltpu.VMEM(wind_speed.shape, f32),
            pltpu.VMEM(wind_dir.shape, f32),
            pltpu.VMEM(ice_mask.shape, jnp.int32),
            pltpu.VMEM(depth_class.shape, jnp.int32),
            pltpu.SMEM(sea_slots.shape, jnp.int32),
            pltpu.SMEM(sea_count.shape, jnp.int32),
            pltpu.SMEM(bottom_table.shape, f32),
            pltpu.SMEM(frequency_table().shape, f32),
            pltpu.SMEM(direction_table().shape, f32),
            dma((9,)),
            pltpu.VMEM((own + 2 * REACH, NF + 2 * PAD, nrow, ncol), f32),
            pltpu.VMEM((own, NF, nrow, ncol), f32),
            pltpu.VMEM((own, NF, nrow, ncol), f32),
            pltpu.VMEM((own, NF, 1, ncol), f32),
            pltpu.VMEM((own, NF, 1, ncol), f32),
            pltpu.VMEM((own, NF, nrow, ncol // 2), f32),
            pltpu.VMEM((nspec, 5 * blk_rows, 1, ncol), f32),
            pltpu.VMEM((nspec, 2, nrow, ncol), f32),
            pltpu.VMEM((7, nrow, ncol), f32),
            pltpu.VMEM((NF, nrow, ncol), f32),
            pltpu.VMEM((nrow, ncol), f32),
            dma,
            dma((2 * REACH * PIECES,)),
            dma((2 * REACH * PIECES,)),
            dma((nspec - 1,)),
            dma((nspec - 1,)),
            dma((nspec - 1,)),
            dma((nspec - 1,)),
            dma((own,)),
            dma((own,)),
            dma((own,)),
            dma((own,)),
            dma((own,)),
        ],
        compiler_params=pltpu.CompilerParams(
            collective_id=0, has_side_effects=True, vmem_limit_bytes=56 * 2**20
        ),
    )(
        spectrum.reshape(own, NF, nrow, ncol),
        wind_speed,
        wind_dir,
        ice_mask,
        depth_class,
        sea_slots,
        sea_count,
        bottom_table,
        jnp.asarray(frequency_table()),
        jnp.asarray(direction_table()),
    )
    return moved.reshape(comps, nrow, ncol)


def step(shape, spectrum, *rest):
    comps, nrow, ncol = spectrum.shape
    fits = (
        shape["spec"] == 4
        and comps * 4 == ND * NF
        and shape["band"] == 2
        and shape["sub"] == 2
        and nrow % 8 == 0
        and ncol % 256 == 0
    )
    return (halo_body if fits else body)(spectrum, *rest)


def solution(mesh):
    return jax.shard_map(
        functools.partial(step, dict(mesh.shape)),
        mesh=mesh,
        in_specs=(
            P(("groups", "spec"), "band", "sub"),
            P(("groups", "band"), "sub", "spec", None),
            P(("groups", "band"), "sub", "spec", None),
            P(("groups", "band"), "sub", "spec", None),
            P(("groups", "band"), "sub", "spec", None),
            P(),
            P(("groups", "band"), "sub", "spec", None),
            P(("groups", "band"), "sub", "spec", None),
        ),
        out_specs=P(("groups", "spec"), "band", "sub"),
        check_vma=False,
    )
```
